32 devices in a mesh: section: 2 (over x), dp: 4 (over y, core), tensor: 4 (over z).
Axes of the slice: x: 2, y: 2, z: 4, core: 2. Of those that a mesh axis runs over, the one named last changes fastest.
Arguments:
- inputs: bfloat16 [2, 4352, 768], P(None, ('dp', 'tensor')), may hold values from -6 to 6
- cotangent: bfloat16 [2, 4352, 768], P(None, ('dp', 'tensor')), may hold values from -6 to 6
- lengths: int32 [2, 4, 3], P(None, 'dp'), may hold values from 1 to 1024, as said below
- routes: int32 [2, 2, 4352, 1], P('section', None, 'dp'), may hold values from 0 to 3; in each aligned block of 1088 rows (0 to 1087, 1088 to 2175, ..., all dimensions but the last counted through in order) at most 544 rows name the same one
- attn_gain: bfloat16 [2, 768], P('section', 'dp'), may hold values from 0.5 to 1.5
- moe_gain: bfloat16 [2, 768], P('section', 'dp'), may hold values from 0.5 to 1.5
- qkv_weight: bfloat16 [2, 768, 3, 768], P('section', 'dp', None, 'tensor'), may hold values from -0.078125 to 0.078125
- out_weight: bfloat16 [2, 768, 768], P('section', 'dp', 'tensor'), may hold values from -3.5 to 3.5
- bias_table: bfloat16 [2, 32, 12], P('section', 'dp', 'tensor'), may hold values from -4 to 4
- router: bfloat16 [2, 768, 4], P('section', 'dp'), may hold values from -0.15625 to 0.15625
- expert_up: bfloat16 [2, 4, 768, 3072], P('section', 'dp', None, 'tensor'), may hold values from -0.21875 to 0.21875
- expert_down: bfloat16 [2, 4, 3072, 768], P('section', 'dp', 'tensor'), may hold values from -0.4375 to 0.4375
Outputs:
- layer_outputs: bfloat16 [2, 2, 4352, 768], P('section', None, ('dp', 'tensor'))
- input_grads: bfloat16 [2, 2, 4352, 768], P('section', None, ('dp', 'tensor'))
- attn_gain_grad: float32 [2, 768], P('section', 'dp')
- moe_gain_grad: float32 [2, 768], P('section', 'dp')
- qkv_grad: float32 [2, 768, 3, 768], P('section', 'dp', None, 'tensor')
- out_grad: float32 [2, 768, 768], P('section', 'dp', 'tensor')
- bias_grad: float32 [2, 32, 12], P('section', 'dp', 'tensor')
- router_grad: float32 [2, 768, 4], P('section', 'dp')
- up_grad: float32 [2, 4, 768, 3072], P('section', 'dp', None, 'tensor')
- down_grad: float32 [2, 4, 3072, 768], P('section', 'dp', 'tensor')
The draws below stay inside these ranges and needn't reach their ends.
Inputs may be any that keep to these rules, and one draw needn't show every extreme that they name: The 3 lengths of one group and micro-batch sum to 1088; the first of them is 1024. `routes`: within the 1088 tokens of one group, micro-batch and layer (aligned blocks of 1088 rows), at most 544 name one expert, and in some blocks an expert is named by exactly 544.
All inputs are finite; a program needn't handle non-finite values.
Results may differ from the reference program's by a relative error of at most 0.025.
Values may be sent and summed in bfloat16 or wider, within the bound.
A program may use at most 448 MiB of HBM per device.

```python
import math
import jax
import jax.numpy as jnp
import numpy as np
from jax import lax

D = 768
H = 12
DH = 64
HD = 768
FF = 3072
NB = 32
EXPERTS = 4
TOK_MB = 1088
LONG = 1024
SEQS = 3
MB = 2
CAP = 544
N_DP = 4


def draw_lengths(key, part):
    key = jax.random.fold_in(key, 11)
    remainder = TOK_MB - LONG
    sub_keys = jax.random.split(key, MB * N_DP)

    def one_group(sub_key):
        cut_points = jnp.sort(jax.random.permutation(sub_key, remainder - 1)[:SEQS - 2] + 1).astype(jnp.int32)
        bounds = jnp.concatenate([jnp.zeros((1,), jnp.int32), cut_points, jnp.full((1,), remainder, jnp.int32)])
        return jnp.concatenate([jnp.full((1,), LONG, jnp.int32), bounds[1:] - bounds[:-1]])
    return jax.vmap(one_group)(sub_keys).reshape(MB, N_DP, SEQS).astype(jnp.int32)


def block_levels(own_key, dims, cuts, low, largest):
    factor_of, own = 1.0, jax.random.fold_in(own_key, 6)
    for dim, shards_of in cuts:
        draws = jnp.exp(jax.random.uniform(jax.random.fold_in(own, dim), (shards_of,), jnp.float32, low / len(cuts), largest / len(cuts)))
        factor_of = factor_of * jnp.repeat(draws, dims[dim] // shards_of).reshape([-1 if axis == dim else 1 for axis in range(len(dims))])
    return factor_of


def assign_block(key, own, number, rows, count, top, most, slope):
    sequence = jax.random.permutation(key, count)
    crowded, usual = shares(count, rows * top, most, slope, True), shares(count, rows * top, most, slope, False)
    places = jnp.arange(count)

    def named(tallies, turn):
        used = int((tallies > 0).sum())
        fixed = max(1, used // 4)
        passed = fixed + (places - fixed + turn * (used - fixed)) % max(1, count - fixed)
        return jnp.zeros((count,), jnp.int32).at[sequence[jnp.where(places < fixed, places, passed)]].set(jnp.asarray(tallies, jnp.int32))

    tallies = jnp.where(number % 4 == 0, named(crowded, number // 4), named(usual, number - number // 4 - 1))
    mixed = jax.random.permutation(jax.random.fold_in(own, 3), count)
    donor, receiver = mixed[0:count // 2 * 2:2], mixed[1:count // 2 * 2:2]
    room = jnp.minimum(tallies[donor] - 1, most - tallies[receiver]) // 2
    room = jnp.where((donor == sequence[0]) | (receiver == sequence[0]) | (tallies[receiver] == 0), 0, jnp.maximum(room, 0))
    passed = jax.random.randint(jax.random.fold_in(own, 4), (count // 2,), 0, 1 << 20) % (room + 1)
    tallies = tallies.at[donor].add(-passed).at[receiver].add(passed)
    members = jnp.searchsorted(jnp.cumsum(tallies), jnp.arange(rows * top), side="right").astype(jnp.int32)
    table = members.reshape(top, rows).T
    table = table[jax.random.permutation(jax.random.fold_in(own, 1), rows)]
    turn = jax.random.randint(jax.random.fold_in(own, 2), (rows, 1), 0, top)
    return jnp.take_along_axis(table, (jnp.arange(top)[None, :] + turn) % top, axis=1)


def shares(count, total, reach, slope, full):
    portions = [(1 << 20) // math.isqrt(grade ** slope) + 1 for grade in range(1, count + 1)]
    largest = reach if full else min(reach, max(-(-total // count), total * portions[0] // sum(portions)))
    least = 1 if total - largest >= count - 1 else 0
    holding, rest = [largest] + [least] * (count - 1), total - largest - least * (count - 1)
    while rest > 0:
        free = [i for i in range(1, count) if holding[i] < largest] or [i for i in range(1, count) if holding[i] < reach]
        pool, left = sum([portions[i] for i in free]), rest
        for i in free:
            more = min(reach - holding[i], max(1, left * portions[i] // pool), rest)
            holding[i] = holding[i] + more
            rest = rest - more
    return np.array(holding)


def noise(own_key, extent, scale, reach, cuts=(), kind=jnp.bfloat16):
    result = scale * jax.random.normal(own_key, extent, jnp.float32)
    if cuts:
        result = result * block_levels(own_key, extent, cuts, -0.22, 0.18)
    return jnp.clip(result, -reach, reach).astype(kind)


def setup_inputs(seed: int = 0) -> dict:
    keys = jax.random.split(jax.random.key(seed), 13)
    inputs = noise(keys[0], (MB, N_DP * TOK_MB, D), 1.0, 6.0, ((1, 16),))
    cotangent = noise(keys[1], (MB, N_DP * TOK_MB, D), 1.0, 6.0, ((1, 16),))
    lengths = draw_lengths(jax.random.fold_in(keys[12], 71), 0)
    routes_keys = jax.random.split(jax.random.fold_in(keys[3], 1), 2 * MB * (N_DP * TOK_MB) // TOK_MB)
    routes_turns = jax.random.permutation(jax.random.fold_in(keys[3], 3), 2 * MB * (N_DP * TOK_MB) // TOK_MB)
    routes = jax.vmap(lambda own, number: assign_block(jax.random.fold_in(keys[3], 2), own, number, TOK_MB, EXPERTS, 1, CAP, 1))(routes_keys, routes_turns).reshape((2, MB, N_DP * TOK_MB, 1))
    attn_gain = jnp.clip(1.0 + 0.1 * jax.random.normal(keys[4], (2, D), jnp.float32), 0.5, 1.5).astype(jnp.bfloat16)
    moe_gain = jnp.clip(1.0 + 0.1 * jax.random.normal(keys[5], (2, D), jnp.float32), 0.5, 1.5).astype(jnp.bfloat16)
    qkv_weight = noise(keys[6], (2, D, 3, HD), (D * 8) ** -0.5, 0.078125, ((0, 2), (1, 4), (3, 4)))
    out_weight = noise(keys[7], (2, D, HD), 3 ** -0.5, 3.5, ((0, 2), (1, 4), (2, 4)))
    bias_table = noise(keys[8], (2, NB, H), 1.0, 4.0, ((0, 2), (1, 4), (2, 4)))
    router = noise(keys[9], (2, D, EXPERTS), (2 * D) ** -0.5, 0.15625, ((0, 2), (1, 4)))
    expert_up = noise(keys[10], (2, EXPERTS, D, FF), D ** -0.5, 0.21875, ((0, 2), (1, 4), (3, 4)))
    expert_down = noise(keys[11], (2, EXPERTS, FF, D), (max(1, FF // (EXPERTS * EXPERTS))) ** -0.5, 0.4375, ((0, 2), (1, 4), (2, 4)))
    return {"inputs": inputs, "cotangent": cotangent, "lengths": lengths, "routes": routes, "attn_gain": attn_gain, "moe_gain": moe_gain, "qkv_weight": qkv_weight, "out_weight": out_weight, "bias_table": bias_table, "router": router, "expert_up": expert_up, "expert_down": expert_down}


EPSILON = 1e-06
HIGHEST = lax.Precision.HIGHEST
THRESHOLDS = np.array([12, 16, 23, 32, 46, 64, 91], dtype=np.int32)

@jax.custom_vjp
def low(v):
    return lax.optimization_barrier(v.astype(jnp.bfloat16)).astype(jnp.float32)

@jax.custom_vjp
def low_back(v):
    return v

def low_keep(v):
    return (low(v), None)

def low_pass(kept, grad):
    return (grad,)

def back_keep(v):
    return (v, None)

def back_low(kept, grad):
    return (low(grad),)
low.defvjp(low_keep, low_pass)
low_back.defvjp(back_keep, back_low)

def bucket_of(distance):
    magnitude = jnp.abs(distance).astype(jnp.int32)
    far_part = 8 + lax.optimization_barrier(jnp.sum((magnitude[..., None] >= jnp.asarray(THRESHOLDS)).astype(jnp.int32), axis=-1))
    nearby = jnp.where(magnitude < 8, magnitude, far_part)
    return (nearby + 16 * (distance > 0).astype(jnp.int32)).astype(jnp.int32)

def rms_norm(values, norm_gain):
    return values * lax.rsqrt(lax.optimization_barrier(jnp.mean(values * values, axis=-1, keepdims=True)) + EPSILON) * norm_gain

def group_attention(normed, segment, qkv_mat, out_mat, rel_table):
    group_rows = normed.shape[0]
    packed = low_back(low(jnp.einsum('td,dch->tch', normed, qkv_mat, precision=HIGHEST)))
    queries = packed[:, 0].reshape(group_rows, H, DH)
    key_rows = packed[:, 1].reshape(group_rows, H, DH)
    val_rows = packed[:, 2].reshape(group_rows, H, DH)
    places = jnp.arange(group_rows, dtype=jnp.int32)
    rel_bias = jnp.take(rel_table, bucket_of(places[None, :] - places[:, None]), axis=0)
    scores = low_back(jnp.einsum('qhe,khe->hqk', queries, key_rows, precision=HIGHEST) + jnp.transpose(rel_bias, (2, 0, 1)))
    scores = jnp.where((segment[:, None] == segment[None, :])[None], scores, -1000000000.0)
    row_max = lax.optimization_barrier(jnp.max(scores, axis=-1, keepdims=True))
    expsum = jnp.exp(scores - row_max)
    chances = expsum / lax.optimization_barrier(jnp.sum(expsum, axis=-1, keepdims=True))
    blended = low_back(low(jnp.einsum('hqk,khe->qhe', low(chances), val_rows, precision=HIGHEST)))
    return low_back(jnp.dot(blended.reshape(group_rows, HD), out_mat.T, precision=HIGHEST))

def expert_block(expert_items):
    rows_in, up_mat, down_mat = expert_items
    pre_act = low_back(jnp.dot(rows_in, up_mat, precision=HIGHEST))
    hidden = low(jax.nn.gelu(pre_act, approximate=True))
    return low_back(low(jnp.dot(hidden, down_mat, precision=HIGHEST)))

def encoder_layer(residual, weights, route_ids, segments):
    attn_scale, moe_scale, qkv_mat, out_mat, rel_table, router_mat, up_mat, down_mat = weights
    groups = MB * N_DP
    normed = low(rms_norm(residual, attn_scale))

    def attend(group_items):
        return group_attention(group_items[0], group_items[1], qkv_mat, out_mat, rel_table)
    attended = lax.map(jax.checkpoint(attend), (normed.reshape(groups, TOK_MB, D), segments.reshape(groups, TOK_MB)))
    middle = residual + attended.reshape(residual.shape)
    branch = low(rms_norm(middle, moe_scale))
    logits = jnp.dot(branch, router_mat, precision=HIGHEST)
    shifted = jnp.exp(logits - lax.optimization_barrier(jnp.max(logits, axis=-1, keepdims=True)))
    chances = shifted / lax.optimization_barrier(jnp.sum(shifted, axis=-1, keepdims=True))
    choose = (route_ids[..., None] == jnp.arange(EXPERTS, dtype=jnp.int32)).astype(jnp.int32)
    gate_value = lax.optimization_barrier(jnp.sum(chances * choose.astype(chances.dtype), axis=-1))
    counted = jnp.cumsum(choose, axis=2)
    slot_index = lax.optimization_barrier(jnp.sum(counted * choose, axis=-1)) - 1
    group_ids = jnp.arange(groups, dtype=jnp.int32).reshape(MB, N_DP, 1)
    target = (route_ids * (groups * CAP) + group_ids * CAP + slot_index).astype(jnp.int32).reshape(-1)
    expert_in = low_back(branch)
    buffer = jnp.zeros((EXPERTS * groups * CAP, D), branch.dtype).at[target].set(expert_in.reshape(-1, D))
    expert_out = lax.map(jax.checkpoint(expert_block), (buffer.reshape(EXPERTS, groups * CAP, D), up_mat, down_mat))
    returned = expert_out.reshape(-1, D)[target].reshape(middle.shape)
    return middle + gate_value[..., None] * returned

def reference(inputs, cotangent, lengths, routes, attn_gain, moe_gain, qkv_weight, out_weight, bias_table, router, expert_up, expert_down):
    places = jnp.arange(TOK_MB, dtype=jnp.int32)
    seq_ends = jnp.cumsum(lengths, axis=-1).astype(jnp.int32)
    segments = lax.optimization_barrier(jnp.sum((places[None, None, :, None] >= seq_ends[:, :, None, :]).astype(jnp.int32), axis=-1)).astype(jnp.int32)
    first_rows = inputs.astype(jnp.float32).reshape(MB, N_DP, TOK_MB, D)
    params = (attn_gain.astype(jnp.float32), moe_gain.astype(jnp.float32), qkv_weight.astype(jnp.float32), out_weight.astype(jnp.float32), bias_table.astype(jnp.float32), router.astype(jnp.float32), expert_up.astype(jnp.float32), expert_down.astype(jnp.float32))
    route_table = routes[..., 0].reshape(2, MB, N_DP, TOK_MB).astype(jnp.int32)

    def forward(first_in, probe_add, layer_params):
        first_params = tuple((item[0] for item in layer_params))
        second_params = tuple((item[1] for item in layer_params))
        first_out = encoder_layer(first_in, first_params, route_table[0], segments)
        second_in = low_back(low(first_out)) + probe_add
        second_out = encoder_layer(second_in, second_params, route_table[1], segments)
        return (second_out, first_out)
    second_out, pullback, first_out = jax.vjp(forward, first_rows, jnp.zeros_like(first_rows), params, has_aux=True)
    grad_first, grad_probe, grad_params = pullback(cotangent.astype(jnp.float32).reshape(first_rows.shape))
    shape_out = (MB, N_DP * TOK_MB, D)
    outputs = jnp.stack([low(first_out).reshape(shape_out), second_out.reshape(shape_out)]).astype(jnp.bfloat16)
    in_grads = jnp.stack([grad_first.reshape(shape_out), grad_probe.reshape(shape_out)]).astype(jnp.bfloat16)
    return (outputs, in_grads, grad_params[0], grad_params[1], grad_params[2], grad_params[3], grad_params[4], grad_params[5], grad_params[6], grad_params[7])
```

```python
import jax
import jax.numpy as jnp
import numpy as np
from jax import lax
from jax.sharding import PartitionSpec as P

LONG = 1024


EPSILON = 1e-06
HIGHEST = lax.Precision.HIGHEST
TILE = 128
THRESHOLDS = np.array([12, 16, 23, 32, 46, 64, 91], dtype=np.int32)


def bucket_of(distance):
    magnitude = jnp.abs(distance)
    far_part = 8 + jnp.sum(
        (magnitude[..., None] >= jnp.asarray(THRESHOLDS)).astype(jnp.int32), axis=-1
    )
    nearby = jnp.where(magnitude < 8, magnitude, far_part)
    return nearby + 16 * (distance > 0).astype(jnp.int32)


def rms_apply(values, norm_gain):
    return (
        values * lax.rsqrt(jnp.mean(values * values, axis=-1, keepdims=True) + EPSILON) * norm_gain
    )


def gelu_apply(values):
    return jax.nn.gelu(values, approximate=True)


def gather_rows(piece):
    return lax.all_gather(piece, "tensor", axis=0, tiled=True)


def sum_rows(piece):
    return lax.psum_scatter(
        piece.astype(jnp.bfloat16), "tensor", scatter_dimension=0, tiled=True
    ).astype(jnp.float32)


def exchange(piece):
    return lax.all_to_all(piece, "dp", split_axis=0, concat_axis=0, tiled=True)


def swap_section(piece):
    return lax.ppermute(piece, "section", [(0, 1), (1, 0)])


def to_second(piece):
    return lax.ppermute(piece, "section", [(0, 1)])


def to_first(piece):
    return lax.ppermute(piece, "section", [(1, 0)])


def band_buckets():
    place = jnp.arange(TILE, dtype=jnp.int32)
    offset = (jnp.arange(3, dtype=jnp.int32) - 1) * TILE
    return bucket_of(offset[:, None, None] + place[None, None, :] - place[None, :, None])


def far_buckets():
    far = bucket_of(jnp.array([-TILE - 1, TILE + 1], dtype=jnp.int32))
    return far[0], far[1]


def relative_bias(rel_table):
    bucket_count, head_count = rel_table.shape
    buckets = band_buckets()
    table = rel_table.astype(jnp.float32).T
    choose = buckets[None, None] == jnp.arange(bucket_count, dtype=jnp.int32)[
        None, :, None, None, None
    ]
    band = jnp.sum(jnp.where(choose, table[:, :, None, None, None], 0.0), axis=1)
    band = band.astype(jnp.bfloat16)
    below, above = far_buckets()
    blocks = LONG // TILE
    shape = (head_count, TILE, (blocks - 2) * TILE)

    def far(number):
        value = jnp.sum(
            jnp.where(
                jnp.arange(bucket_count, dtype=jnp.int32)[None, :] == number, table, 0.0
            ),
            axis=1,
        ).astype(jnp.bfloat16)
        return jnp.broadcast_to(value[:, None, None], shape)

    strip = jnp.concatenate([far(below), band[:, 0], band[:, 1], band[:, 2], far(above)], axis=2)
    rows = [
        strip[:, :, (blocks - 1 - block) * TILE : (2 * blocks - 1 - block) * TILE]
        for block in range(blocks)
    ]
    return jnp.concatenate(rows, axis=1)


def bias_sums(head_grad, tail_grad, bucket_count):
    blocks = LONG // TILE
    tail = tail_grad.shape[1]

    def tile(row, column):
        return head_grad[
            :, row * TILE : (row + 1) * TILE, column * TILE : (column + 1) * TILE
        ].astype(jnp.float32)

    left = sum(tile(block, block - 1) for block in range(1, blocks))
    middle = sum(tile(block, block) for block in range(blocks))
    right = sum(tile(block, block + 1) for block in range(blocks - 1))
    middle = middle + jnp.pad(
        tail_grad.astype(jnp.float32), ((0, 0), (0, TILE - tail), (0, TILE - tail))
    )
    band = jnp.stack([left, middle, right], axis=1)
    numbers = jnp.arange(bucket_count, dtype=jnp.int32)
    choose = band_buckets()[None] == numbers[:, None, None, None]
    table = jnp.sum(jnp.where(choose[:, None], band[None], 0.0), axis=(2, 3, 4))
    block_of = jnp.arange(LONG, dtype=jnp.int32) // TILE
    apart = block_of[None, :] - block_of[:, None]
    wide = head_grad.astype(jnp.float32)
    low_sum = jnp.sum(jnp.where((apart <= -2)[None], wide, 0.0), axis=(1, 2))
    high_sum = jnp.sum(jnp.where((apart >= 2)[None], wide, 0.0), axis=(1, 2))
    below, above = far_buckets()
    table = table + jnp.where((numbers == below)[:, None], low_sum[None], 0.0)
    return table + jnp.where((numbers == above)[:, None], high_sum[None], 0.0)


def attend_scores(packed, rel_bias, allowed):
    scores = (
        jnp.einsum("qhe,khe->hqk", packed[:, 0], packed[:, 1], preferred_element_type=jnp.float32)
        + rel_bias
    )
    if allowed is None:
        return scores
    return jnp.where(allowed[None], scores, -1000000000.0)


def attend_forward(packed, rel_bias, allowed):
    scores = attend_scores(packed, rel_bias, allowed)
    row_max = jnp.max(scores, axis=-1, keepdims=True)
    expsum = jnp.exp(scores - row_max)
    total = jnp.sum(expsum, axis=-1, keepdims=True)
    chances = expsum / total
    log_total = row_max[..., 0] + jnp.log(total[..., 0])
    blended = jnp.einsum(
        "hqk,khe->qhe",
        chances.astype(jnp.bfloat16),
        packed[:, 2],
        preferred_element_type=jnp.float32,
    )
    return (blended.astype(jnp.bfloat16), log_total)


def attend_backward(packed, rel_bias, allowed, log_total, grad_blend):
    scores = attend_scores(packed, rel_bias, allowed)
    chances = jnp.exp(scores - log_total[..., None])
    grad_chance = jnp.einsum(
        "qhe,khe->hqk", grad_blend, packed[:, 2], preferred_element_type=jnp.float32
    )
    inner = jnp.sum(chances * grad_chance, axis=-1, keepdims=True)
    grad_score = (chances * (grad_chance - inner)).astype(jnp.bfloat16)
    grad_query = jnp.einsum(
        "hqk,khe->qhe", grad_score, packed[:, 1], preferred_element_type=jnp.float32
    )
    grad_key = jnp.einsum(
        "hqk,qhe->khe", grad_score, packed[:, 0], preferred_element_type=jnp.float32
    )
    grad_value = jnp.einsum(
        "hqk,qhe->khe", chances.astype(jnp.bfloat16), grad_blend, preferred_element_type=jnp.float32
    )
    grad_packed = jnp.stack([grad_query, grad_key, grad_value], axis=1).astype(jnp.bfloat16)
    return (grad_packed, grad_score)


def split_forward(packed, rel_bias, allowed):
    tail = packed.shape[0] - LONG
    head_blend, head_log = attend_forward(packed[:LONG], rel_bias, None)
    tail_blend, tail_log = attend_forward(packed[LONG:], rel_bias[:, :tail, :tail], allowed)
    return (jnp.concatenate([head_blend, tail_blend], axis=0), (head_log, tail_log))


def split_backward(packed, rel_bias, allowed, logs, grad_blend, bucket_count):
    tail = packed.shape[0] - LONG
    head_grad, head_scores = attend_backward(
        packed[:LONG], rel_bias, None, logs[0], grad_blend[:LONG]
    )
    tail_grad, tail_scores = attend_backward(
        packed[LONG:], rel_bias[:, :tail, :tail], allowed, logs[1], grad_blend[LONG:]
    )
    grad_table = bias_sums(head_scores, tail_scores, bucket_count)
    return (jnp.concatenate([head_grad, tail_grad], axis=0), grad_table)


def route_target(route_ids, experts, capacity):
    rows = route_ids.shape[0]
    choose = route_ids[:, None] == jnp.arange(experts, dtype=jnp.int32)[None, :]
    place = jnp.arange(rows, dtype=jnp.int32)
    earlier = (place[:, None] >= place[None, :]).astype(jnp.bfloat16)
    counted = jnp.dot(earlier, choose.astype(jnp.bfloat16), preferred_element_type=jnp.float32)
    slot = jnp.sum(jnp.where(choose, counted, 0.0), axis=1).astype(jnp.int32) - 1
    return route_ids * capacity + slot


def body(
    inputs,
    cotangent,
    lengths,
    routes,
    attn_gain,
    moe_gain,
    qkv_weight,
    out_weight,
    bias_table,
    router,
    expert_up,
    expert_down,
):
    section_pos = lax.axis_index("section")
    tensor_pos = lax.axis_index("tensor")
    tensor_count = lax.axis_size("tensor")
    dp_count = lax.axis_size("dp")
    batches, local_rows, model_dim = inputs.shape
    layers = lax.axis_size("section")
    group_rows = local_rows * tensor_count
    experts = router.shape[-1]
    capacity = 2 * group_rows // experts
    slots = capacity * experts
    assert batches == layers == 2 and expert_up.shape[1] == 1 and experts == dp_count
    first = section_pos == 0
    part = model_dim // dp_count
    head_feats = qkv_weight.shape[3]
    bucket_part, head_count = bias_table.shape[1:]
    bucket_count = bucket_part * dp_count
    head_dim = head_feats // head_count
    packed_feats = 3 * head_feats

    small = jnp.concatenate(
        [attn_gain[0], moe_gain[0], router[0].reshape(-1), bias_table[0].reshape(-1)]
    )
    smalls = lax.all_gather(small, ("section", "dp"), axis=0).reshape(layers, dp_count, -1)
    large = jnp.concatenate([qkv_weight[0].reshape(part, packed_feats), out_weight[0]], axis=1)
    larges = lax.all_gather(large, ("section", "dp"), axis=0, tiled=True)
    larges = larges.reshape(layers, model_dim, -1)
    all_routes = lax.all_gather(routes, "section", axis=0, tiled=True)
    other_up = swap_section(expert_up[0, 0])
    other_down = swap_section(expert_down[0, 0])
    up_mats = (
        jnp.where(first, expert_up[0, 0], other_up),
        jnp.where(first, other_up, expert_up[0, 0]),
    )
    down_mats = (
        jnp.where(first, expert_down[0, 0], other_down),
        jnp.where(first, other_down, expert_down[0, 0]),
    )

    seq_ends = jnp.cumsum(lax.dynamic_index_in_dim(lengths[:, 0], section_pos, 0, keepdims=False))
    places = jnp.arange(LONG, group_rows, dtype=jnp.int32)
    segment = jnp.sum((places[:, None] >= seq_ends[None, :]).astype(jnp.int32), axis=-1)
    allowed = segment[:, None] == segment[None, :]
    places_all = jnp.arange(slots, dtype=jnp.int32)

    def layer_setup(layer):
        route_ids = lax.dynamic_index_in_dim(all_routes[layer], section_pos, 0, keepdims=False)[:, 0]
        target = route_target(route_ids, experts, capacity)
        own_route = lax.dynamic_slice_in_dim(route_ids, tensor_pos * local_rows, local_rows)
        own_choose = (
            own_route[:, None] == jnp.arange(experts, dtype=jnp.int32)[None, :]
        ).astype(jnp.float32)
        scales = smalls[layer]
        attn_scale = scales[:, :part].reshape(-1).astype(jnp.float32)
        moe_scale = scales[:, part : 2 * part].reshape(-1).astype(jnp.float32)
        router_end = (2 + experts) * part
        router_mat = scales[:, 2 * part : router_end].reshape(model_dim, experts)
        rel_table = scales[:, router_end:].reshape(bucket_count, head_count)
        qkv_mat = larges[layer][:, :packed_feats]
        out_mat = larges[layer][:, packed_feats:]
        rel_bias = relative_bias(rel_table)
        return (target, own_choose, attn_scale, moe_scale, router_mat, qkv_mat, out_mat, rel_bias)

    def to_experts(own_rows, target):
        chosen = (places_all[:, None] == target[None, :]).astype(jnp.bfloat16)
        outgoing = jnp.dot(
            chosen, gather_rows(own_rows), preferred_element_type=jnp.float32
        ).astype(jnp.bfloat16)
        return exchange(outgoing.reshape(experts, capacity, model_dim)).reshape(-1, model_dim)

    def from_experts(produced, target):
        produced = produced.astype(jnp.bfloat16).reshape(experts, capacity, model_dim)
        returned = exchange(produced).reshape(slots, model_dim)
        chosen = (target[:, None] == places_all[None, :]).astype(jnp.bfloat16)
        own = jnp.dot(chosen, returned, preferred_element_type=jnp.float32)
        return sum_rows(own)

    def layer_forward(layer_in, setting, up_mat, down_mat):
        target, own_choose, attn_scale, moe_scale, router_mat, qkv_mat, out_mat, rel_bias = setting
        residual = layer_in.astype(jnp.float32)
        normed = rms_apply(residual, attn_scale).astype(jnp.bfloat16)
        normed_full = gather_rows(normed)
        packed = jnp.dot(normed_full, qkv_mat, preferred_element_type=jnp.float32)
        packed = packed.astype(jnp.bfloat16).reshape(group_rows, 3, head_count, head_dim)
        packed, up_mat, down_mat = lax.optimization_barrier((packed, up_mat, down_mat))
        blended, logs = split_forward(packed, rel_bias, allowed)
        attn_full = lax.dot_general(
            blended.reshape(group_rows, -1),
            out_mat,
            (((1,), (1,)), ((), ())),
            preferred_element_type=jnp.float32,
        )
        middle = residual + sum_rows(attn_full)
        branch = rms_apply(middle, moe_scale).astype(jnp.bfloat16)
        logits = jnp.dot(branch, router_mat, preferred_element_type=jnp.float32)
        received = to_experts(branch, target)
        pre_act = jnp.dot(received, up_mat, preferred_element_type=jnp.float32)
        hidden = gelu_apply(pre_act).astype(jnp.bfloat16)
        produced = jnp.dot(hidden, down_mat, preferred_element_type=jnp.float32)
        own_out = from_experts(produced, target).astype(jnp.bfloat16)
        chances = jax.nn.softmax(logits, axis=-1)
        gate_value = jnp.sum(chances * own_choose, axis=-1)
        result = (middle + gate_value[:, None] * own_out.astype(jnp.float32)).astype(jnp.bfloat16)
        stored = (
            residual,
            normed_full,
            packed,
            logs,
            blended,
            middle,
            branch,
            logits,
            own_out,
            received,
            pre_act,
            hidden,
        )
        return (result, stored)

    def layer_backward(grad_in, setting, stored, up_mat, down_mat, send, arrived):
        target, own_choose, attn_scale, moe_scale, router_mat, qkv_mat, out_mat, rel_bias = setting
        (
            residual,
            normed_full,
            packed,
            logs,
            blended,
            middle,
            branch,
            logits,
            own_out,
            received,
            pre_act,
            hidden,
        ) = stored
        grad_out = grad_in.astype(jnp.float32)

        def gate_of(logit_rows):
            return jnp.sum(jax.nn.softmax(logit_rows, axis=-1) * own_choose, axis=-1)

        gate_value, gate_pull = jax.vjp(gate_of, logits)
        grad_gate = jnp.sum(grad_out * own_out.astype(jnp.float32), axis=-1)
        grad_eo = (gate_value[:, None] * grad_out).astype(jnp.bfloat16)
        grad_prod = to_experts(grad_eo, target)
        grad_hidden = lax.dot_general(
            grad_prod, down_mat, (((1,), (1,)), ((), ())), preferred_element_type=jnp.float32
        )
        unused_value, gelu_pull = jax.vjp(gelu_apply, pre_act)
        grad_pre = gelu_pull(grad_hidden)[0].astype(jnp.bfloat16)
        grad_input = lax.dot_general(
            grad_pre, up_mat, (((1,), (1,)), ((), ())), preferred_element_type=jnp.float32
        )
        grad_down = lax.dot_general(
            hidden, grad_prod, (((0,), (0,)), ((), ())), preferred_element_type=jnp.float32
        )
        grad_up = lax.dot_general(
            received, grad_pre, (((0,), (0,)), ((), ())), preferred_element_type=jnp.float32
        )
        sent_up, sent_down = grad_up.astype(jnp.bfloat16), grad_down.astype(jnp.bfloat16)
        grad_input, sent_up, sent_down = lax.optimization_barrier(
            (grad_input, sent_up, sent_down)
        )
        sent_up, sent_down = send(sent_up), send(sent_down)
        grad_branch_e = from_experts(grad_input, target)
        grad_logits = gate_pull(grad_gate)[0]
        grad_branch = grad_branch_e + jnp.dot(
            grad_logits, router_mat.astype(jnp.float32).T, precision=HIGHEST
        )
        grad_router = jnp.dot(branch.astype(jnp.float32).T, grad_logits, precision=HIGHEST)
        unused_middle, norm_pull = jax.vjp(rms_apply, middle, moe_scale)
        grad_mid_norm, grad_moe_scale = norm_pull(grad_branch)
        grad_middle = grad_out + grad_mid_norm
        grad_attn = gather_rows(grad_middle.astype(jnp.bfloat16))
        grad_blend = jnp.dot(grad_attn, out_mat, preferred_element_type=jnp.float32).astype(
            jnp.bfloat16
        )
        if arrived is not None:
            grad_blend, arrived = lax.optimization_barrier((grad_blend, arrived))
        grad_packed, grad_table = split_backward(
            packed,
            rel_bias,
            allowed,
            logs,
            grad_blend.reshape(group_rows, head_count, head_dim),
            bucket_count,
        )
        flat_grad = grad_packed.reshape(group_rows, -1)
        grad_normed = sum_rows(
            lax.dot_general(
                flat_grad, qkv_mat, (((1,), (1,)), ((), ())), preferred_element_type=jnp.float32
            )
        )
        grad_out_mat = lax.dot_general(
            grad_attn,
            blended.reshape(group_rows, -1),
            (((0,), (0,)), ((), ())),
            preferred_element_type=jnp.float32,
        )
        grad_qkv = lax.dot_general(
            normed_full, flat_grad, (((0,), (0,)), ((), ())), preferred_element_type=jnp.float32
        )
        unused_resid, norm_pull_attn = jax.vjp(rms_apply, residual, attn_scale)
        grad_res_norm, grad_attn_scale = norm_pull_attn(grad_normed)
        grad_resid = (grad_middle + grad_res_norm).astype(jnp.bfloat16)
        grad_large = jnp.concatenate([grad_qkv, grad_out_mat], axis=1)
        grad_small = jnp.concatenate(
            [
                grad_attn_scale.reshape(dp_count, -1),
                grad_moe_scale.reshape(dp_count, -1),
                grad_router.reshape(dp_count, -1),
                grad_table.reshape(dp_count, -1),
            ],
            axis=1,
        )
        width = grad_large.shape[1]
        extra_rows = -(-grad_small.shape[1] // (16 * width)) * 16
        grad_small = jnp.pad(
            grad_small, ((0, 0), (0, extra_rows * width - grad_small.shape[1]))
        ).reshape(dp_count, extra_rows, width)
        grad_large = jnp.concatenate(
            [grad_large.reshape(dp_count, part, width), grad_small], axis=1
        ).astype(jnp.bfloat16)
        return (grad_resid, grad_large, sent_up, sent_down, grad_up, grad_down, arrived)

    settings = (layer_setup(0), layer_setup(1))
    layer_in = lax.dynamic_index_in_dim(inputs, section_pos, 0, keepdims=False)
    out0, stored0 = layer_forward(layer_in, settings[0], up_mats[0], down_mats[0])
    out1, stored1 = layer_forward(out0, settings[1], up_mats[1], down_mats[1])
    grad_in = lax.dynamic_index_in_dim(cotangent, section_pos, 0, keepdims=False)
    res1, large1, got_up1, got_down1, up1, down1, unused = layer_backward(
        grad_in, settings[1], stored1, up_mats[1], down_mats[1], to_second, None
    )
    res1, large1 = lax.optimization_barrier((res1, large1))
    got_large1 = to_second(large1)
    res0, large0, got_up0, got_down0, up0, down0, arrived = layer_backward(
        res1,
        settings[0],
        stored0,
        up_mats[0],
        down_mats[0],
        to_first,
        (got_up1, got_down1, got_large1),
    )
    got_up1, got_down1, got_large1 = arrived
    got_large0 = to_first(large0)

    def place(rows0, rows1):
        from_second = to_first(rows0)
        from_first = to_second(rows1)
        return jnp.where(
            first, jnp.stack([rows0, from_second]), jnp.stack([from_first, rows1])
        )[None]

    def total(grad0, grad1, from_second, from_first):
        from_second = from_second.astype(jnp.float32)
        from_first = from_first.astype(jnp.float32)
        return jnp.where(first, grad0 + from_second, grad1 + from_first)

    layer_outputs = place(out0, out1)
    input_grads = place(res0, res1)
    up_total = total(up0, up1, got_up0, got_up1)
    down_total = total(down0, down1, got_down0, got_down1)
    large_total = total(large0, large1, got_large0, got_large1).astype(jnp.bfloat16)
    large_total = lax.psum_scatter(large_total, "dp", scatter_dimension=0, tiled=True)[0]
    large_total = large_total.astype(jnp.float32)
    small_total = large_total[part:].reshape(-1)
    large_total = large_total[:part]
    router_end = (2 + experts) * part
    table_end = router_end + bucket_part * head_count
    table_total = small_total[router_end:table_end].reshape(bucket_part, head_count)
    small_total = lax.psum(small_total[:router_end], "tensor")
    return (
        layer_outputs,
        input_grads,
        small_total[:part][None],
        small_total[part : 2 * part][None],
        large_total[:, :packed_feats].reshape(part, 3, head_feats)[None],
        large_total[:, packed_feats:][None],
        table_total[None],
        small_total[2 * part : router_end].reshape(part, experts)[None],
        up_total[None, None],
        down_total[None, None],
    )


def solution(mesh):
    placed = (
        P(None, ("dp", "tensor"), None),
        P(None, ("dp", "tensor"), None),
        P(None, "dp", None),
        P("section", None, "dp", None),
        P("section", "dp"),
        P("section", "dp"),
        P("section", "dp", None, "tensor"),
        P("section", "dp", "tensor"),
        P("section", "dp", "tensor"),
        P("section", "dp", None),
        P("section", "dp", None, "tensor"),
        P("section", "dp", "tensor", None),
    )
    return jax.shard_map(
        body,
        mesh=mesh,
        in_specs=placed,
        out_specs=(
            P("section", None, ("dp", "tensor"), None),
            P("section", None, ("dp", "tensor"), None),
            P("section", "dp"),
            P("section", "dp"),
            P("section", "dp", None, "tensor"),
            P("section", "dp", "tensor"),
            P("section", "dp", "tensor"),
            P("section", "dp", None),
            P("section", "dp", None, "tensor"),
            P("section", "dp", "tensor", None),
        ),
        check_vma=False,
    )
```

```python
import jax
import jax.numpy as jnp
import numpy as np
from jax import lax
from jax.sharding import PartitionSpec as P

LONG = 1024


EPSILON = 1e-06
HIGHEST = lax.Precision.HIGHEST
TILE = 128
THRESHOLDS = np.array([12, 16, 23, 32, 46, 64, 91], dtype=np.int32)


def bucket_of(distance):
    magnitude = jnp.abs(distance)
    far_part = 8 + jnp.sum(
        (magnitude[..., None] >= jnp.asarray(THRESHOLDS)).astype(jnp.int32), axis=-1
    )
    nearby = jnp.where(magnitude < 8, magnitude, far_part)
    return nearby + 16 * (distance > 0).astype(jnp.int32)


def rms_apply(values, norm_gain):
    return (
        values * lax.rsqrt(jnp.mean(values * values, axis=-1, keepdims=True) + EPSILON) * norm_gain
    )


def gelu_apply(values):
    return jax.nn.gelu(values, approximate=True)


def gather_rows(piece):
    return lax.all_gather(piece, "tensor", axis=0, tiled=True)


def sum_rows(piece):
    return lax.psum_scatter(
        piece.astype(jnp.bfloat16), "tensor", scatter_dimension=0, tiled=True
    ).astype(jnp.float32)


def exchange(piece):
    return lax.all_to_all(piece, "dp", split_axis=0, concat_axis=0, tiled=True)


def swap_section(piece):
    return lax.ppermute(piece, "section", [(0, 1), (1, 0)])


def to_second(piece):
    return lax.ppermute(piece, "section", [(0, 1)])


def to_first(piece):
    return lax.ppermute(piece, "section", [(1, 0)])


def band_buckets():
    place = jnp.arange(TILE, dtype=jnp.int32)
    offset = (jnp.arange(3, dtype=jnp.int32) - 1) * TILE
    return bucket_of(offset[:, None, None] + place[None, None, :] - place[None, :, None])


def far_buckets():
    far = bucket_of(jnp.array([-TILE - 1, TILE + 1], dtype=jnp.int32))
    return far[0], far[1]


def relative_bias(rel_table):
    bucket_count, head_count = rel_table.shape
    buckets = band_buckets()
    table = rel_table.astype(jnp.float32).T
    choose = buckets[None, None] == jnp.arange(bucket_count, dtype=jnp.int32)[
        None, :, None, None, None
    ]
    band = jnp.sum(jnp.where(choose, table[:, :, None, None, None], 0.0), axis=1)
    band = band.astype(jnp.bfloat16)
    below, above = far_buckets()
    blocks = LONG // TILE
    shape = (head_count, TILE, (blocks - 2) * TILE)

    def far(number):
        value = jnp.sum(
            jnp.where(
                jnp.arange(bucket_count, dtype=jnp.int32)[None, :] == number, table, 0.0
            ),
            axis=1,
        ).astype(jnp.bfloat16)
        return jnp.broadcast_to(value[:, None, None], shape)

    strip = jnp.concatenate([far(below), band[:, 0], band[:, 1], band[:, 2], far(above)], axis=2)
    rows = [
        strip[:, :, (blocks - 1 - block) * TILE : (2 * blocks - 1 - block) * TILE]
        for block in range(blocks)
    ]
    return jnp.concatenate(rows, axis=1)


def bias_sums(head_grad, tail_grad, bucket_count):
    blocks = LONG // TILE
    tail = tail_grad.shape[1]

    def tile(row, column):
        return head_grad[
            :, row * TILE : (row + 1) * TILE, column * TILE : (column + 1) * TILE
        ].astype(jnp.float32)

    left = sum(tile(block, block - 1) for block in range(1, blocks))
    middle = sum(tile(block, block) for block in range(blocks))
    right = sum(tile(block, block + 1) for block in range(blocks - 1))
    middle = middle + jnp.pad(
        tail_grad.astype(jnp.float32), ((0, 0), (0, TILE - tail), (0, TILE - tail))
    )
    band = jnp.stack([left, middle, right], axis=1)
    numbers = jnp.arange(bucket_count, dtype=jnp.int32)
    choose = band_buckets()[None] == numbers[:, None, None, None]
    table = jnp.sum(jnp.where(choose[:, None], band[None], 0.0), axis=(2, 3, 4))
    block_of = jnp.arange(LONG, dtype=jnp.int32) // TILE
    apart = block_of[None, :] - block_of[:, None]
    wide = head_grad.astype(jnp.float32)
    low_sum = jnp.sum(jnp.where((apart <= -2)[None], wide, 0.0), axis=(1, 2))
    high_sum = jnp.sum(jnp.where((apart >= 2)[None], wide, 0.0), axis=(1, 2))
    below, above = far_buckets()
    table = table + jnp.where((numbers == below)[:, None], low_sum[None], 0.0)
    return table + jnp.where((numbers == above)[:, None], high_sum[None], 0.0)


def attend_scores(packed, rel_bias, allowed):
    scores = (
        jnp.einsum("qhe,khe->hqk", packed[:, 0], packed[:, 1], preferred_element_type=jnp.float32)
        + rel_bias
    )
    if allowed is None:
        return scores
    return jnp.where(allowed[None], scores, -1000000000.0)


def attend_forward(packed, rel_bias, allowed):
    scores = attend_scores(packed, rel_bias, allowed)
    row_max = jnp.max(scores, axis=-1, keepdims=True)
    expsum = jnp.exp(scores - row_max)
    total = jnp.sum(expsum, axis=-1, keepdims=True)
    chances = expsum / total
    log_total = row_max[..., 0] + jnp.log(total[..., 0])
    blended = jnp.einsum(
        "hqk,khe->qhe",
        chances.astype(jnp.bfloat16),
        packed[:, 2],
        preferred_element_type=jnp.float32,
    )
    return (blended.astype(jnp.bfloat16), log_total)


def attend_backward(packed, rel_bias, allowed, log_total, grad_blend):
    scores = attend_scores(packed, rel_bias, allowed)
    chances = jnp.exp(scores - log_total[..., None])
    grad_chance = jnp.einsum(
        "qhe,khe->hqk", grad_blend, packed[:, 2], preferred_element_type=jnp.float32
    )
    inner = jnp.sum(chances * grad_chance, axis=-1, keepdims=True)
    grad_score = (chances * (grad_chance - inner)).astype(jnp.bfloat16)
    grad_query = jnp.einsum(
        "hqk,khe->qhe", grad_score, packed[:, 1], preferred_element_type=jnp.float32
    )
    grad_key = jnp.einsum(
        "hqk,qhe->khe", grad_score, packed[:, 0], preferred_element_type=jnp.float32
    )
    grad_value = jnp.einsum(
        "hqk,qhe->khe", chances.astype(jnp.bfloat16), grad_blend, preferred_element_type=jnp.float32
    )
    grad_packed = jnp.stack([grad_query, grad_key, grad_value], axis=1).astype(jnp.bfloat16)
    return (grad_packed, grad_score)


def split_forward(packed, rel_bias, allowed):
    tail = packed.shape[0] - LONG
    head_blend, head_log = attend_forward(packed[:LONG], rel_bias, None)
    tail_blend, tail_log = attend_forward(packed[LONG:], rel_bias[:, :tail, :tail], allowed)
    return (jnp.concatenate([head_blend, tail_blend], axis=0), (head_log, tail_log))


def split_backward(packed, rel_bias, allowed, logs, grad_blend, bucket_count):
    tail = packed.shape[0] - LONG
    head_grad, head_scores = attend_backward(
        packed[:LONG], rel_bias, None, logs[0], grad_blend[:LONG]
    )
    tail_grad, tail_scores = attend_backward(
        packed[LONG:], rel_bias[:, :tail, :tail], allowed, logs[1], grad_blend[LONG:]
    )
    grad_table = bias_sums(head_scores, tail_scores, bucket_count)
    return (jnp.concatenate([head_grad, tail_grad], axis=0), grad_table)


def route_target(route_ids, experts, capacity):
    rows = route_ids.shape[0]
    choose = route_ids[:, None] == jnp.arange(experts, dtype=jnp.int32)[None, :]
    place = jnp.arange(rows, dtype=jnp.int32)
    earlier = (place[:, None] >= place[None, :]).astype(jnp.bfloat16)
    counted = jnp.dot(earlier, choose.astype(jnp.bfloat16), preferred_element_type=jnp.float32)
    slot = jnp.sum(jnp.where(choose, counted, 0.0), axis=1).astype(jnp.int32) - 1
    return route_ids * capacity + slot


def body(
    inputs,
    cotangent,
    lengths,
    routes,
    attn_gain,
    moe_gain,
    qkv_weight,
    out_weight,
    bias_table,
    router,
    expert_up,
    expert_down,
):
    section_pos = lax.axis_index("section")
    tensor_pos = lax.axis_index("tensor")
    tensor_count = lax.axis_size("tensor")
    dp_count = lax.axis_size("dp")
    batches, local_rows, model_dim = inputs.shape
    layers = lax.axis_size("section")
    group_rows = local_rows * tensor_count
    experts = router.shape[-1]
    capacity = 2 * group_rows // experts
    slots = capacity * experts
    assert batches == layers == 2 and expert_up.shape[1] == 1 and experts == dp_count
    first = section_pos == 0
    part = model_dim // dp_count
    head_feats = qkv_weight.shape[3]
    bucket_part, head_count = bias_table.shape[1:]
    bucket_count = bucket_part * dp_count
    head_dim = head_feats // head_count
    packed_feats = 3 * head_feats

    small = jnp.concatenate(
        [attn_gain[0], moe_gain[0], router[0].reshape(-1), bias_table[0].reshape(-1)]
    )
    smalls = lax.all_gather(small, ("section", "dp"), axis=0).reshape(layers, dp_count, -1)
    large = jnp.concatenate([qkv_weight[0].reshape(part, packed_feats), out_weight[0]], axis=1)
    larges = lax.all_gather(large, ("section", "dp"), axis=0, tiled=True)
    larges = larges.reshape(layers, model_dim, -1)
    all_routes = lax.all_gather(routes, "section", axis=0, tiled=True)
    other_up = swap_section(expert_up[0, 0])
    other_down = swap_section(expert_down[0, 0])
    up_mats = (
        jnp.where(first, expert_up[0, 0], other_up),
        jnp.where(first, other_up, expert_up[0, 0]),
    )
    down_mats = (
        jnp.where(first, expert_down[0, 0], other_down),
        jnp.where(first, other_down, expert_down[0, 0]),
    )

    seq_ends = jnp.cumsum(lax.dynamic_index_in_dim(lengths[:, 0], section_pos, 0, keepdims=False))
    places = jnp.arange(LONG, group_rows, dtype=jnp.int32)
    segment = jnp.sum((places[:, None] >= seq_ends[None, :]).astype(jnp.int32), axis=-1)
    allowed = segment[:, None] == segment[None, :]
    places_all = jnp.arange(slots, dtype=jnp.int32)

    def layer_setup(layer):
        route_ids = lax.dynamic_index_in_dim(all_routes[layer], section_pos, 0, keepdims=False)[:, 0]
        target = route_target(route_ids, experts, capacity)
        own_route = lax.dynamic_slice_in_dim(route_ids, tensor_pos * local_rows, local_rows)
        own_choose = (
            own_route[:, None] == jnp.arange(experts, dtype=jnp.int32)[None, :]
        ).astype(jnp.float32)
        scales = smalls[layer]
        attn_scale = scales[:, :part].reshape(-1).astype(jnp.float32)
        moe_scale = scales[:, part : 2 * part].reshape(-1).astype(jnp.float32)
        router_end = (2 + experts) * part
        router_mat = scales[:, 2 * part : router_end].reshape(model_dim, experts)
        rel_table = scales[:, router_end:].reshape(bucket_count, head_count)
        qkv_mat = larges[layer][:, :packed_feats]
        out_mat = larges[layer][:, packed_feats:]
        rel_bias = relative_bias(rel_table)
        return (target, own_choose, attn_scale, moe_scale, router_mat, qkv_mat, out_mat, rel_bias)

    def to_experts(own_rows, target):
        chosen = (places_all[:, None] == target[None, :]).astype(jnp.bfloat16)
        outgoing = jnp.dot(
            chosen, gather_rows(own_rows), preferred_element_type=jnp.float32
        ).astype(jnp.bfloat16)
        return exchange(outgoing.reshape(experts, capacity, model_dim)).reshape(-1, model_dim)

    def from_experts(produced, target, beside=()):
        produced = produced.astype(jnp.bfloat16).reshape(experts, capacity, model_dim)
        returned = exchange(produced)
        returned, beside = lax.optimization_barrier((returned, beside))
        returned = returned.reshape(slots, model_dim)
        chosen = (target[:, None] == places_all[None, :]).astype(jnp.bfloat16)
        own = jnp.dot(chosen, returned, preferred_element_type=jnp.float32)
        return sum_rows(own), beside

    def layer_forward(layer_in, setting, up_mat, down_mat):
        target, own_choose, attn_scale, moe_scale, router_mat, qkv_mat, out_mat, rel_bias = setting
        residual = layer_in.astype(jnp.float32)
        normed = rms_apply(residual, attn_scale).astype(jnp.bfloat16)
        normed_full = gather_rows(normed)
        packed = jnp.dot(normed_full, qkv_mat, preferred_element_type=jnp.float32)
        packed = packed.astype(jnp.bfloat16).reshape(group_rows, 3, head_count, head_dim)
        blended, logs = split_forward(packed, rel_bias, allowed)
        attn_full = lax.dot_general(
            blended.reshape(group_rows, -1),
            out_mat,
            (((1,), (1,)), ((), ())),
            preferred_element_type=jnp.float32,
        )
        middle = residual + sum_rows(attn_full)
        branch = rms_apply(middle, moe_scale).astype(jnp.bfloat16)
        logits = jnp.dot(branch, router_mat, preferred_element_type=jnp.float32)
        received = to_experts(branch, target)
        received, up_mat, down_mat = lax.optimization_barrier((received, up_mat, down_mat))
        pre_act = jnp.dot(received, up_mat, preferred_element_type=jnp.float32)
        hidden = gelu_apply(pre_act).astype(jnp.bfloat16)
        produced = jnp.dot(hidden, down_mat, preferred_element_type=jnp.float32)
        own_out = from_experts(produced, target)[0].astype(jnp.bfloat16)
        chances = jax.nn.softmax(logits, axis=-1)
        gate_value = jnp.sum(chances * own_choose, axis=-1)
        result = (middle + gate_value[:, None] * own_out.astype(jnp.float32)).astype(jnp.bfloat16)
        stored = (
            residual,
            normed_full,
            packed,
            logs,
            blended,
            middle,
            branch,
            logits,
            own_out,
            received,
            pre_act,
            hidden,
        )
        return (result, stored)

    def layer_backward(grad_in, setting, stored, up_mat, down_mat, send):
        target, own_choose, attn_scale, moe_scale, router_mat, qkv_mat, out_mat, rel_bias = setting
        (
            residual,
            normed_full,
            packed,
            logs,
            blended,
            middle,
            branch,
            logits,
            own_out,
            received,
            pre_act,
            hidden,
        ) = stored
        grad_out = grad_in.astype(jnp.float32)

        def gate_of(logit_rows):
            return jnp.sum(jax.nn.softmax(logit_rows, axis=-1) * own_choose, axis=-1)

        gate_value, gate_pull = jax.vjp(gate_of, logits)
        grad_gate = jnp.sum(grad_out * own_out.astype(jnp.float32), axis=-1)
        grad_eo = (gate_value[:, None] * grad_out).astype(jnp.bfloat16)
        grad_prod = to_experts(grad_eo, target)
        grad_hidden = lax.dot_general(
            grad_prod, down_mat, (((1,), (1,)), ((), ())), preferred_element_type=jnp.float32
        )
        unused_value, gelu_pull = jax.vjp(gelu_apply, pre_act)
        grad_pre = gelu_pull(grad_hidden)[0].astype(jnp.bfloat16)
        grad_input = lax.dot_general(
            grad_pre, up_mat, (((1,), (1,)), ((), ())), preferred_element_type=jnp.float32
        )
        grad_down = lax.dot_general(
            hidden, grad_prod, (((0,), (0,)), ((), ())), preferred_element_type=jnp.float32
        )
        grad_up = lax.dot_general(
            received, grad_pre, (((0,), (0,)), ((), ())), preferred_element_type=jnp.float32
        )
        sent_up, sent_down = grad_up.astype(jnp.bfloat16), grad_down.astype(jnp.bfloat16)
        grad_input, sent_up, sent_down = lax.optimization_barrier(
            (grad_input, sent_up, sent_down)
        )
        sent_up, sent_down = send(sent_up), send(sent_down)
        grad_branch_e, (sent_up, sent_down) = from_experts(
            grad_input, target, (sent_up, sent_down)
        )
        grad_logits = gate_pull(grad_gate)[0]
        grad_branch = grad_branch_e + jnp.dot(
            grad_logits, router_mat.astype(jnp.float32).T, precision=HIGHEST
        )
        grad_router = jnp.dot(branch.astype(jnp.float32).T, grad_logits, precision=HIGHEST)
        unused_middle, norm_pull = jax.vjp(rms_apply, middle, moe_scale)
        grad_mid_norm, grad_moe_scale = norm_pull(grad_branch)
        grad_middle = grad_out + grad_mid_norm
        grad_attn = gather_rows(grad_middle.astype(jnp.bfloat16))
        grad_blend = jnp.dot(grad_attn, out_mat, preferred_element_type=jnp.float32).astype(
            jnp.bfloat16
        )
        grad_packed, grad_table = split_backward(
            packed,
            rel_bias,
            allowed,
            logs,
            grad_blend.reshape(group_rows, head_count, head_dim),
            bucket_count,
        )
        flat_grad = grad_packed.reshape(group_rows, -1)
        grad_normed = sum_rows(
            lax.dot_general(
                flat_grad, qkv_mat, (((1,), (1,)), ((), ())), preferred_element_type=jnp.float32
            )
        )
        grad_out_mat = lax.dot_general(
            grad_attn,
            blended.reshape(group_rows, -1),
            (((0,), (0,)), ((), ())),
            preferred_element_type=jnp.float32,
        )
        grad_qkv = lax.dot_general(
            normed_full, flat_grad, (((0,), (0,)), ((), ())), preferred_element_type=jnp.float32
        )
        unused_resid, norm_pull_attn = jax.vjp(rms_apply, residual, attn_scale)
        grad_res_norm, grad_attn_scale = norm_pull_attn(grad_normed)
        grad_resid = (grad_middle + grad_res_norm).astype(jnp.bfloat16)
        grad_large = jnp.concatenate([grad_qkv, grad_out_mat], axis=1)
        grad_small = jnp.concatenate(
            [
                grad_attn_scale.reshape(dp_count, -1),
                grad_moe_scale.reshape(dp_count, -1),
                grad_router.reshape(dp_count, -1),
                grad_table.reshape(dp_count, -1),
            ],
            axis=1,
        )
        width = grad_large.shape[1]
        extra_rows = -(-grad_small.shape[1] // (16 * width)) * 16
        grad_small = jnp.pad(
            grad_small, ((0, 0), (0, extra_rows * width - grad_small.shape[1]))
        ).reshape(dp_count, extra_rows, width)
        grad_large = jnp.concatenate(
            [grad_large.reshape(dp_count, part, width), grad_small], axis=1
        ).astype(jnp.bfloat16)
        return (grad_resid, grad_large, sent_up, sent_down, grad_up, grad_down)

    settings = (layer_setup(0), layer_setup(1))
    layer_in = lax.dynamic_index_in_dim(inputs, section_pos, 0, keepdims=False)
    out0, stored0 = layer_forward(layer_in, settings[0], up_mats[0], down_mats[0])
    out1, stored1 = layer_forward(out0, settings[1], up_mats[1], down_mats[1])
    grad_in = lax.dynamic_index_in_dim(cotangent, section_pos, 0, keepdims=False)
    res1, large1, got_up1, got_down1, up1, down1 = layer_backward(
        grad_in, settings[1], stored1, up_mats[1], down_mats[1], to_second
    )
    large1 = lax.psum_scatter(large1, "dp", scatter_dimension=0, tiled=True)
    got_large1 = to_second(large1)
    res0, large0, got_up0, got_down0, up0, down0 = layer_backward(
        res1, settings[0], stored0, up_mats[0], down_mats[0], to_first
    )
    large0 = lax.psum_scatter(large0, "dp", scatter_dimension=0, tiled=True)
    got_large0 = to_first(large0)

    def place(rows0, rows1):
        from_second = to_first(rows0)
        from_first = to_second(rows1)
        return jnp.where(
            first, jnp.stack([rows0, from_second]), jnp.stack([from_first, rows1])
        )[None]

    def total(grad0, grad1, from_second, from_first):
        from_second = from_second.astype(jnp.float32)
        from_first = from_first.astype(jnp.float32)
        return jnp.where(
            first,
            grad0.astype(jnp.float32) + from_second,
            grad1.astype(jnp.float32) + from_first,
        )

    layer_outputs = place(out0, out1)
    input_grads = place(res0, res1)
    up_total = total(up0, up1, got_up0, got_up1)
    down_total = total(down0, down1, got_down0, got_down1)
    large_total = total(large0, large1, got_large0, got_large1)[0]
    small_total = large_total[part:].reshape(-1)
    large_total = large_total[:part]
    router_end = (2 + experts) * part
    table_end = router_end + bucket_part * head_count
    table_total = small_total[router_end:table_end].reshape(bucket_part, head_count)
    small_total = lax.psum(small_total[:router_end], "tensor")
    return (
        layer_outputs,
        input_grads,
        small_total[:part][None],
        small_total[part : 2 * part][None],
        large_total[:, :packed_feats].reshape(part, 3, head_feats)[None],
        large_total[:, packed_feats:][None],
        table_total[None],
        small_total[2 * part : router_end].reshape(part, experts)[None],
        up_total[None, None],
        down_total[None, None],
    )


def solution(mesh):
    placed = (
        P(None, ("dp", "tensor"), None),
        P(None, ("dp", "tensor"), None),
        P(None, "dp", None),
        P("section", None, "dp", None),
        P("section", "dp"),
        P("section", "dp"),
        P("section", "dp", None, "tensor"),
        P("section", "dp", "tensor"),
        P("section", "dp", "tensor"),
        P("section", "dp", None),
        P("section", "dp", None, "tensor"),
        P("section", "dp", "tensor", None),
    )
    return jax.shard_map(
        body,
        mesh=mesh,
        in_specs=placed,
        out_specs=(
            P("section", None, ("dp", "tensor"), None),
            P("section", None, ("dp", "tensor"), None),
            P("section", "dp"),
            P("section", "dp"),
            P("section", "dp", None, "tensor"),
            P("section", "dp", "tensor"),
            P("section", "dp", "tensor"),
            P("section", "dp", None),
            P("section", "dp", None, "tensor"),
            P("section", "dp", "tensor", None),
        ),
        check_vma=False,
    )
```
